256 devices in a mesh: dp: 64 (over y, z, core), grp: 4 (over x).
Axes of the slice: x: 4, y: 4, z: 8, core: 2. Of those that a mesh axis runs over, the one named last changes fastest.
Arguments:
- embeddings: bfloat16 [196608, 768], P(('dp', 'grp'))
- cluster_ids: int32 [196608], P(('dp', 'grp')), may hold values from 0 to 511, as said below
Outputs:
- max_similarity: float32 [196608], P(('dp', 'grp'))
The draws below stay inside these ranges and needn't reach their ends.
Inputs may be any that keep to these rules, and one draw needn't show every extreme that they name: `cluster_ids`: within the rows of one device, at most 24 rows belong to the clusters of any one group (cluster c belongs to group c // 8); in every draw some group receives exactly 24 rows from every device.
All inputs are finite; a program needn't handle non-finite values.
Results may differ from the reference program's by a relative error of at most 0.0003.
Values may be sent and summed in bfloat16 or wider, within the bound.
A program may use at most 64 MiB of HBM per device.

```python
import math
import jax
import jax.numpy as jnp
from jax import lax

D = 768
R_DEV = 768
CL_GRP = 8
CAP = 24
ROWS = 196608
N_DP = 64
N_GRP = 4


def layout(key):
    first_key = jax.random.fold_in(key, 101)
    favored = jax.random.randint(first_key, (), 0, N_DP)
    block_base = jax.random.fold_in(key, 102)

    def one_block(block):
        block_key = jax.random.fold_in(block_base, block)
        key_slots, key_order, key_local = jax.random.split(block_key, 3)
        slots = jax.random.permutation(key_slots, (N_DP - 1) * CAP)[:R_DEV - CAP]
        index = slots // CAP
        others = (index + (index >= favored).astype(jnp.int32)).astype(jnp.int32)
        owners = jnp.concatenate([jnp.full((CAP,), favored, jnp.int32), others])
        owners = jax.random.permutation(key_order, owners)
        local = jax.random.randint(key_local, (R_DEV,), 0, CL_GRP)
        return (owners * CL_GRP + local).astype(jnp.int32)
    return jax.vmap(one_block)(jnp.arange(N_DP * N_GRP, dtype=jnp.int32)).reshape(-1)


def draw_cluster_ids(key, part):
    labels = layout(key)
    return labels


def draw_embeddings(key, part):
    labels = layout(key)
    key = jax.random.fold_in(key, 7)
    key_center = jax.random.fold_in(key, 0)
    key_item = jax.random.fold_in(key, 1)
    key_weight = jax.random.fold_in(key, 2)
    key_noise = jax.random.fold_in(key, 3)
    key_pick = jax.random.fold_in(key, 5)
    spread = max(2, R_DEV * N_GRP // (2 * CL_GRP))
    picks = jax.random.randint(key_pick, (ROWS,), 0, spread)
    items = labels * spread + picks
    centers = jax.vmap(lambda label: jax.random.normal(jax.random.fold_in(key_center, label), (D,)))(labels)
    vectors = jax.vmap(lambda item: jax.random.normal(jax.random.fold_in(key_item, item), (D,)))(items)
    fraction = jax.vmap(lambda item: jax.random.uniform(jax.random.fold_in(key_weight, item), ()))(items)
    strength = jnp.exp(math.log(0.3) + fraction * math.log(4.0 / 0.3))
    noise = jax.random.normal(key_noise, (ROWS, D))
    values = noise + 0.6 * centers + strength[:, None] * vectors
    return values.astype(jnp.bfloat16)


def setup_inputs(seed: int = 0) -> dict:
    key_list = jax.random.split(jax.random.key(seed), 3)
    embeddings = draw_embeddings(jax.random.fold_in(key_list[2], 71), 0)
    cluster_ids = draw_cluster_ids(jax.random.fold_in(key_list[2], 71), 0)
    return dict(embeddings=embeddings, cluster_ids=cluster_ids)


def unit_scale(block):
    values = block.astype(jnp.float32)
    return lax.rsqrt(lax.optimization_barrier(jnp.mean(values * values, axis=1)) + 1e-06) / math.sqrt(block.shape[1])

def reference(embeddings, cluster_ids):
    owners = (cluster_ids // CL_GRP).astype(jnp.int32)
    group_range = jnp.arange(N_DP, dtype=jnp.int32)
    counts = lax.optimization_barrier(jnp.sum((owners[:, None] == group_range[None, :]).astype(jnp.int32), axis=0)).astype(jnp.int32)
    starts = (jnp.cumsum(counts) - counts).astype(jnp.int32)
    order = jnp.argsort(owners, stable=True).astype(jnp.int32)
    span = N_DP * CAP * N_GRP
    positions = jnp.arange(span, dtype=jnp.int32)

    def per_owner(group):
        valid = positions < counts[group]
        index = jnp.where(valid, starts[group] + positions, 0).astype(jnp.int32)
        chosen = order[index]
        block = embeddings[chosen]
        scale = unit_scale(block)
        labels = jnp.where(valid, cluster_ids[chosen], -1)
        products = jnp.dot(block, block.T, preferred_element_type=jnp.float32)
        cosines = products * scale[:, None] * scale[None, :]
        same = (labels[:, None] == labels[None, :]) & (labels[:, None] >= 0)
        same = same & (positions[:, None] != positions[None, :])
        best_sim = lax.optimization_barrier(jnp.max(jnp.where(same, cosines, -1.0), axis=1))
        target = jnp.where(valid, chosen, ROWS).astype(jnp.int32)
        return (best_sim, target)
    best_all, target_all = lax.map(per_owner, group_range)
    result = jnp.zeros((ROWS,), best_all.dtype)
    return result.at[target_all.reshape(-1)].set(best_all.reshape(-1), mode='drop')
```

```python
import math

import jax
import jax.numpy as jnp
from jax import lax
from jax.experimental import pallas as pl
from jax.experimental.pallas import tpu as pltpu
from jax.sharding import PartitionSpec as P

D = 768
RD = 768
G = 64
CAP = 24
NCH = 8
SRC = 16
B = SRC * CAP
MESH = pl.DeviceIdType.MESH
F32, BF16 = jnp.float32, jnp.bfloat16


def place(x, y, z, c):
    return ((y * 8 + z) * 2 + c, x)


def local_wait(ref, sem):
    pltpu.make_async_copy(ref, ref, sem).wait()


def pair_max(v, scale_col, id_col, scale_row, id_row, itself=None):
    row, cols = None, []
    for t in range(v.shape[1] // 128):
        at = slice(128 * t, 128 * (t + 1))
        same = id_col == id_row[:, at]
        if itself is not None:
            same = same & ~itself[:, at]
        m = jnp.where(same, v[:, at] * scale_col * scale_row[:, at], -1.0)
        row = m if row is None else jnp.maximum(row, m)
        cols.append(jnp.max(m, axis=0, keepdims=True))
    return row, jnp.concatenate(cols, axis=1)


def nt(a, b):
    return lax.dot_general(a, b, (((1,), (1,)), ((), ())), preferred_element_type=F32)


def kernel(
    ids_ref, emb_ref, out_ref,
    send, idsend, onehot, lanes, recv, idrecv, joint, meta, colmax, theirs, answer, back, scol, icol, rowmax,
    s_rows, s_ids, r_rows, r_ids, s_joint, s_meta, r_joint, r_meta, s_part, r_part, s_ans, r_ans,
):
    dp, x = lax.axis_index("dp"), lax.axis_index("grp")
    y, z, c = dp // 16, (dp // 2) % 8, dp % 2
    zh, par = z // 2, z % 2
    owner = (x + y + z) % 2 == 0
    other = place(x, y, z, 1 - c)

    barrier = pltpu.get_barrier_semaphore()

    @pl.when(owner)
    def _():
        @pl.loop(1, 128)
        def _(t):
            d = place((x + t // 32) % 4, (y + t // 8) % 4, (z + t) % 8, c)
            pl.semaphore_signal(barrier, inc=1, device_id=d, device_id_type=MESH)

        pl.semaphore_signal(barrier, inc=1, device_id=other, device_id_type=MESH)

    ids = ids_ref[...]
    g = ids // 8
    rel = ((g // 16 - x) & 3) * 16 + ((g // 4 - y) & 3) * 4 + ((g - zh) & 3)
    hot = (lax.broadcasted_iota(jnp.int32, (G, RD), 0) == rel).astype(F32)
    onehot[...] = hot
    before = (
        lax.broadcasted_iota(jnp.int32, (RD, RD), 0) < lax.broadcasted_iota(jnp.int32, (RD, RD), 1)
    ).astype(F32).astype(BF16)
    counts = jnp.dot(hot.astype(BF16), before, preferred_element_type=F32)
    rank = jnp.sum(counts * hot, axis=0, keepdims=True).astype(jnp.int32)
    slot = rel * CAP + rank
    lane = ((rel & 7) * 2 + par) * CAP + rank
    at_lane = (lax.broadcasted_iota(jnp.int32, (B, RD), 0) == lane).astype(F32).astype(BF16)
    lanes[...] = at_lane
    idsend[:, 0, :] = nt((hot * ((ids & 7) + 1).astype(F32)).astype(BF16), at_lane)

    pl.semaphore_wait(barrier, 64)

    def row_copy(i):
        tx, ty, th = (x + i // 16) % 4, (y + i // 4) % 4, (zh + i) % 4
        to = place(tx, ty, 2 * th + (tx + ty) % 2, c)
        k, s = i // 8, 2 * i + par
        return (
            pltpu.make_async_remote_copy(
                send.at[pl.ds(3 * i, 3)], recv.at[pl.ds(3 * s, 3)], s_rows, r_rows.at[k],
                device_id=to, device_id_type=MESH),
            pltpu.make_async_remote_copy(
                idsend.at[i], idrecv.at[s], s_ids, r_ids.at[k], device_id=to, device_id_type=MESH),
        )

    @pl.loop(0, NCH)
    def _(q):
        pick = lax.broadcasted_iota(jnp.int32, (8 * CAP, RD), 0) + q * (8 * CAP) == slot
        rows = jnp.dot(pick.astype(F32).astype(BF16), emb_ref[...], preferred_element_type=F32)
        send[pl.ds(q * 24, 24)] = rows.astype(BF16).reshape(24, 8, D)

        @pl.loop(0, 8)
        def _(n):
            i = q * 8 + n
            mine = jnp.logical_and(owner, i == 0)

            @pl.when(jnp.logical_not(mine))
            def _():
                for copy in row_copy(i):
                    copy.start()

            @pl.when(mine)
            def _():
                pltpu.make_async_copy(send.at[pl.ds(0, 3)], recv.at[pl.ds(3 * par, 3)], r_rows.at[0]).start()
                pltpu.make_async_copy(idsend.at[0], idrecv.at[par], r_ids.at[0]).start()

    @pl.when(owner)
    def _():
        colmax[...] = jnp.full(colmax.shape, -1.0, F32)

        @pl.loop(0, NCH)
        def _(k):
            chunk = recv.at[pl.ds(k * 48, 48)]
            local_wait(chunk, r_rows.at[k])
            joint[k, pl.ds(0, B), :] = chunk[...].reshape(B, D)
            pltpu.make_async_remote_copy(
                joint.at[k, pl.ds(0, B)], joint.at[k, pl.ds(B, B)], s_joint, r_joint.at[k],
                device_id=other, device_id_type=MESH).start()
            local_wait(idrecv.at[pl.ds(k * SRC, SRC)], r_ids.at[k])
            id_row = jnp.max(idrecv[pl.ds(k * SRC, SRC)], axis=0)
            mine = joint[k, pl.ds(0, B), :]
            gram = nt(mine, mine)
            eye = lax.broadcasted_iota(jnp.int32, (B, B), 0) == lax.broadcasted_iota(jnp.int32, (B, B), 1)
            squares = jnp.where(eye, gram, 0.0)
            scale_row = lax.rsqrt(jnp.sum(squares, axis=0, keepdims=True) / D + 1e-6) / math.sqrt(D)
            scale_col = lax.rsqrt(jnp.sum(squares, axis=1, keepdims=True) / D + 1e-6) / math.sqrt(D)
            id_col = jnp.sum(jnp.where(eye, id_row, 0.0), axis=1, keepdims=True)
            meta[k, 0, :, pl.ds(0, B)] = id_row
            meta[k, 1, :, pl.ds(0, B)] = scale_row
            pltpu.make_async_remote_copy(
                meta.at[k, :, :, pl.ds(0, B)], meta.at[k, :, :, pl.ds(B, B)], s_meta, r_meta.at[k],
                device_id=other, device_id_type=MESH).start()
            scol[...] = jnp.broadcast_to(scale_col, (B, 128))
            icol[...] = jnp.broadcast_to(id_col, (B, 128))
            row, _ = pair_max(gram, scol[...], icol[...], scale_row, id_row, eye)
            rowmax[...] = row

            @pl.loop(0, k)
            def _(j):
                for n in range(3):
                    at = pl.ds(256 * n, 256)
                    v = nt(joint[k, pl.ds(0, B), :], joint[j, at, :])
                    row, col = pair_max(v, scol[...], icol[...], meta[j, 1, :, at], meta[j, 0, :, at])
                    rowmax[...] = jnp.maximum(rowmax[...], row)
                    colmax[j, :, at] = jnp.maximum(colmax[j, :, at], col)

            local_wait(joint.at[k, pl.ds(B, B)], r_joint.at[k])
            local_wait(meta.at[k, :, :, pl.ds(B, B)], r_meta.at[k])
            v = nt(joint[k, pl.ds(0, B), :], joint[k, pl.ds(B, B), :])
            row, _ = pair_max(v, scol[...], icol[...], meta[k, 1, :, pl.ds(B, B)], meta[k, 0, :, pl.ds(B, B)])
            row = jnp.maximum(rowmax[...], row)
            best = jnp.max(row.T, axis=0, keepdims=True)
            colmax[k, :, pl.ds(0, B)] = jnp.maximum(colmax[k, :, pl.ds(0, B)], best)

        part = pltpu.make_async_remote_copy(
            colmax.at[:, :, pl.ds(B, B)], theirs, s_part, r_part, device_id=other, device_id_type=MESH)
        part.start()
        part.wait()
        answer[...] = jnp.maximum(colmax[:, :, pl.ds(0, B)], theirs[...])

        @pl.loop(0, 2 * G)
        def _(s):
            i, p = s // 2, s % 2
            mine = jnp.logical_and(i == 0, p == par)
            to = place((x - i // 16 + 4) % 4, (y - (i // 4) % 4 + 4) % 4, 2 * ((zh - i % 4 + 4) % 4) + p, c)

            @pl.when(jnp.logical_not(mine))
            def _():
                pltpu.make_async_remote_copy(
                    answer.at[i // 8], back.at[i], s_ans, r_ans, device_id=to, device_id_type=MESH).start()

            @pl.when(mine)
            def _():
                pltpu.make_async_copy(answer.at[0], back.at[0], r_ans).start()

        local_wait(joint.at[:, pl.ds(0, B)], s_joint)
        local_wait(meta.at[:, :, :, pl.ds(0, B)], s_meta)
        local_wait(idrecv.at[pl.ds(0, 127)], s_ans)
        local_wait(send.at[pl.ds(0, 189)], s_rows)
        local_wait(idsend.at[pl.ds(0, 63)], s_ids)

    @pl.when(jnp.logical_not(owner))
    def _():
        local_wait(send, s_rows)
        local_wait(idsend, s_ids)

    local_wait(back, r_ans)
    rest = back[:, 0, :]
    total = None
    for _ in range(3):
        term = rest.astype(BF16)
        rest = rest - term.astype(F32)
        found = jnp.dot(term, lanes[...], preferred_element_type=F32)
        total = found if total is None else total + found
    out_ref[...] = jnp.sum(total * onehot[...], axis=0, keepdims=True)


def on_device(embeddings, cluster_ids):
    dma = pltpu.SemaphoreType.DMA
    best = pl.pallas_call(
        kernel,
        out_shape=jax.ShapeDtypeStruct((1, RD), F32),
        in_specs=[pl.BlockSpec(memory_space=pltpu.VMEM)] * 2,
        out_specs=pl.BlockSpec(memory_space=pltpu.VMEM),
        scratch_shapes=[
            pltpu.VMEM((G * 3, 8, D), BF16),
            pltpu.VMEM((G, 1, B), F32),
            pltpu.VMEM((G, RD), F32),
            pltpu.VMEM((B, RD), BF16),
            pltpu.VMEM((2 * G * 3, 8, D), BF16),
            pltpu.VMEM((2 * G, 1, B), F32),
            pltpu.VMEM((NCH, 2 * B, D), BF16),
            pltpu.VMEM((NCH, 2, 1, 2 * B), F32),
            pltpu.VMEM((NCH, 1, 2 * B), F32),
            pltpu.VMEM((NCH, 1, B), F32),
            pltpu.VMEM((NCH, 1, B), F32),
            pltpu.VMEM((G, 1, B), F32),
            pltpu.VMEM((B, 128), F32),
            pltpu.VMEM((B, 128), F32),
            pltpu.VMEM((B, 128), F32),
            dma, dma, dma((NCH,)), dma((NCH,)), dma, dma, dma((NCH,)), dma((NCH,)), dma, dma, dma, dma,
        ],
        compiler_params=pltpu.CompilerParams(
            collective_id=0, has_side_effects=True, vmem_limit_bytes=48 << 20
        ),
        name="semdedup",
    )(cluster_ids.reshape(1, RD), embeddings)
    return best.reshape(RD)


def solution(mesh):
    placed = (P(("dp", "grp"), None), P(("dp", "grp")))
    return jax.shard_map(
        on_device, mesh=mesh, in_specs=placed, out_specs=P(("dp", "grp")), check_vma=False
    )
```

```python
import math

import jax
import jax.numpy as jnp
from jax import lax
from jax.experimental import pallas as pl
from jax.experimental.pallas import tpu as pltpu
from jax.sharding import PartitionSpec as P

D = 768
RD = 768
G = 64
CAP = 24
NCH = 8
AHEAD = 6
SRC = 16
B = SRC * CAP
MESH = pl.DeviceIdType.MESH
F32, BF16 = jnp.float32, jnp.bfloat16


COLUMNS = (
    (0, 0), (2, 2), (1, 3), (3, 1), (1, 1), (3, 3), (0, 1), (0, 3),
    (1, 0), (3, 0), (0, 2), (2, 0), (1, 2), (3, 2), (2, 1), (2, 3),
)


def offset(t):
    def pick(which):
        out = jnp.int32(0)
        for n, xy in enumerate(COLUMNS):
            if xy[which]:
                out = jnp.where(t == n, xy[which], out)
        return out

    return pick(0), pick(1)


def lookup(dx, dy):
    out = jnp.zeros_like(dx)
    for n, xy in enumerate(COLUMNS):
        out = jnp.where((dx == xy[0]) & (dy == xy[1]), n, out)
    return out


def place(x, y, z, c):
    return ((y * 8 + z) * 2 + c, x)


def local_wait(ref, sem):
    pltpu.make_async_copy(ref, ref, sem).wait()


def pair_max(v, scale_col, id_col, scale_row, id_row, itself=None):
    row, cols = None, []
    for t in range(v.shape[1] // 128):
        at = slice(128 * t, 128 * (t + 1))
        same = id_col == id_row[:, at]
        if itself is not None:
            same = same & ~itself[:, at]
        m = jnp.where(same, v[:, at] * scale_col * scale_row[:, at], -1.0)
        row = m if row is None else jnp.maximum(row, m)
        cols.append(jnp.max(m, axis=0, keepdims=True))
    return row, jnp.concatenate(cols, axis=1)


def nt(a, b):
    return lax.dot_general(a, b, (((1,), (1,)), ((), ())), preferred_element_type=F32)


def kernel(
    ids_hbm, emb_hbm, out_ref,
    ids_ref, emb, send, idsend, idline, idlayer, idrecv, hot, lanes, recv, joint, meta, colmax, half, whole, back,
    scol, icol, rowmax,
    ready, s_in, s_rows, s_ids, s_idl, s_joint, s_meta, s_half, s_whole,
    r_rows, r_ids, r_idl, r_joint, r_meta, r_half, r_whole,
):
    dp, x = lax.axis_index("dp"), lax.axis_index("grp")
    y, z, c = dp // 16, (dp // 2) % 8, dp % 2
    zh, par = z // 2, z % 2
    owner = (x + y + z) % 2 == 0
    me_in_layer = x * 2 + y // 2
    other = place(x, y, z, 1 - c)

    def remote(src, dst, ssem, rsem, to):
        return pltpu.make_async_remote_copy(src, dst, ssem, rsem, device_id=to, device_id_type=MESH)

    def signal(sem, to):
        pl.semaphore_signal(sem, inc=1, device_id=to, device_id_type=MESH)

    get_ids = pltpu.make_async_copy(ids_hbm, ids_ref, s_in.at[0])
    get_ids.start()
    get_emb = pltpu.make_async_copy(emb_hbm, emb, s_in.at[1])
    get_emb.start()

    barrier = pltpu.get_barrier_semaphore()

    @pl.loop(1, 8)
    def _(t):
        signal(barrier, place(x, y, (z + t) % 8, c))

    @pl.when(owner)
    def _():
        signal(barrier, other)

        @pl.loop(1, 16)
        def _(t):
            signal(barrier, place((x + t // 4) % 4, (y + t) % 4, z, c))

    get_ids.wait()
    ids = ids_ref[...].reshape(1, RD)
    g = ids // 8
    gx, gy, gh = g // 16, (g // 4) & 3, g & 3
    col = lookup((gx - x) & 3, (gy - y) & 3)
    dh = (gh - zh) & 3
    line = ((2 * gh + ((gx + gy) & 1) - z) & 7) * 8 + gx * 2 + gy // 2
    mask = (lax.broadcasted_iota(jnp.int32, (G, RD), 0) == line).astype(F32)
    hot[...] = mask
    before = (
        lax.broadcasted_iota(jnp.int32, (RD, RD), 0) < lax.broadcasted_iota(jnp.int32, (RD, RD), 1)
    ).astype(F32).astype(BF16)
    counts = jnp.dot(mask.astype(BF16), before, preferred_element_type=F32)
    rank = jnp.sum(counts * mask, axis=0, keepdims=True).astype(jnp.int32)
    slot = (col * 4 + dh) * CAP + rank
    lane = ((col & 1) * 8 + dh * 2 + par) * CAP + rank
    at_lane = (lax.broadcasted_iota(jnp.int32, (B, RD), 0) == lane).astype(F32).astype(BF16)
    lanes[...] = at_lane
    idsend[:, 0, :] = nt((mask * ((ids & 7) + 1).astype(F32)).astype(BF16), at_lane)

    get_emb.wait()

    @pl.loop(0, NCH)
    def _(q):
        pick = lax.broadcasted_iota(jnp.int32, (8 * CAP, RD), 0) + q * (8 * CAP) == slot
        rows = jnp.dot(pick.astype(F32).astype(BF16), emb[...], preferred_element_type=F32)
        send[pl.ds(q * 24, 24)] = rows.astype(BF16).reshape(24, 8, D)

    pl.semaphore_wait(barrier, 15)

    @pl.loop(1, 8)
    def _(t):
        signal(ready, place(x, y, (z + t) % 8, c))

    @pl.loop(1, 8)
    def _(t):
        remote(idsend.at[pl.ds(8 * t, 8)], idline.at[t - 1], s_ids, r_ids, place(x, y, (z + t) % 8, c)).start()

    def issue(q):
        @pl.loop(0, 8)
        def _(n):
            i = q * 8 + n
            dx, dy = offset(i // 4)
            tx, ty = (x + dx) % 4, (y + dy) % 4
            k, at = i // 8, 2 * i + par
            mine = jnp.logical_and(owner, i == 0)

            @pl.when(jnp.logical_not(mine))
            def _():
                to = place(tx, ty, 2 * ((zh + i) % 4) + (tx + ty) % 2, c)
                remote(send.at[pl.ds(3 * i, 3)], recv.at[pl.ds(3 * at, 3)], s_rows.at[k], r_rows.at[k], to).start()

            @pl.when(mine)
            def _():
                pltpu.make_async_copy(send.at[pl.ds(0, 3)], recv.at[pl.ds(3 * par, 3)], r_rows.at[0]).start()

    def sent(q):
        @pl.when(jnp.logical_and(owner, q == 0))
        def _():
            local_wait(send.at[pl.ds(0, 21)], s_rows.at[0])

        @pl.when(jnp.logical_not(jnp.logical_and(owner, q == 0)))
        def _():
            local_wait(send.at[pl.ds(0, 24)], s_rows.at[q])

    pl.semaphore_wait(ready, 7)

    @pl.loop(0, AHEAD)
    def _(q):
        issue(q)

    local_wait(idline, r_ids)
    idlayer[...] = jnp.maximum(idsend[pl.ds(0, 8)], jnp.max(idline[...], axis=0))

    @pl.loop(0, 16)
    def _(t):
        dx, dy = offset(t)
        tx, ty = (x + dx) % 4, (y + dy) % 4

        @pl.when(jnp.logical_and((tx + ty + z) % 2 == 0, t > 0))
        def _():
            remote(idlayer.at[tx * 2 + ty // 2], idrecv.at[t], s_idl, r_idl, place(tx, ty, z, c)).start()

    @pl.when(jnp.logical_not(owner))
    def _():
        @pl.loop(AHEAD, NCH)
        def _(q):
            sent(q - AHEAD)
            issue(q)

    @pl.when(owner)
    def _():
        colmax[...] = jnp.full(colmax.shape, -1.0, F32)
        idrecv[0] = idlayer[me_in_layer]
        local_wait(idrecv.at[pl.ds(1, 15)], r_idl)

        def finish(k):
            local_wait(joint.at[k, pl.ds(B, B)], r_joint.at[k])
            local_wait(meta.at[k, :, :, pl.ds(B, B)], r_meta.at[k])
            v = nt(joint[k, pl.ds(0, B), :], joint[k, pl.ds(B, B), :])
            at = pl.ds(B, B)
            row, _ = pair_max(v, scol[k % 2], icol[k % 2], meta[k, 1, :, at], meta[k, 0, :, at])
            row = jnp.maximum(rowmax[k % 2], row)
            best = jnp.max(row.T, axis=0, keepdims=True)
            colmax[k, :, pl.ds(0, B)] = jnp.maximum(colmax[k, :, pl.ds(0, B)], best)

        @pl.loop(0, NCH)
        def _(k):
            chunk = recv.at[pl.ds(k * 48, 48)]
            @pl.when(k + AHEAD < NCH)
            def _():
                sent(k)
                issue(k + AHEAD)

            local_wait(chunk, r_rows.at[k])
            joint[k, pl.ds(0, B), :] = chunk[...].reshape(B, D)
            remote(joint.at[k, pl.ds(0, B)], joint.at[k, pl.ds(B, B)], s_joint, r_joint.at[k], other).start()
            id_row = jnp.maximum(idrecv[2 * k], idrecv[2 * k + 1])
            mine = joint[k, pl.ds(0, B), :]
            gram = nt(mine, mine)
            eye = lax.broadcasted_iota(jnp.int32, (B, B), 0) == lax.broadcasted_iota(jnp.int32, (B, B), 1)
            squares = jnp.where(eye, gram, 0.0)
            scale_row = lax.rsqrt(jnp.sum(squares, axis=0, keepdims=True) / D + 1e-6) / math.sqrt(D)
            scale_col = lax.rsqrt(jnp.sum(squares, axis=1, keepdims=True) / D + 1e-6) / math.sqrt(D)
            id_col = jnp.sum(jnp.where(eye, id_row, 0.0), axis=1, keepdims=True)
            meta[k, 0, :, pl.ds(0, B)] = id_row
            meta[k, 1, :, pl.ds(0, B)] = scale_row
            remote(
                meta.at[k, :, :, pl.ds(0, B)], meta.at[k, :, :, pl.ds(B, B)], s_meta, r_meta.at[k], other
            ).start()
            scol[k % 2] = jnp.broadcast_to(scale_col, (B, 128))
            icol[k % 2] = jnp.broadcast_to(id_col, (B, 128))
            row, _ = pair_max(gram, scol[k % 2], icol[k % 2], scale_row, id_row, eye)
            rowmax[k % 2] = row

            @pl.when(k > 0)
            def _():
                finish(k - 1)

            def cross(*chunks):
                best = rowmax[k % 2]
                for j in chunks:
                    for n in range(3):
                        at = pl.ds(256 * n, 256)
                        v = nt(joint[k, pl.ds(0, B), :], joint[j, at, :])
                        row, col = pair_max(v, scol[k % 2], icol[k % 2], meta[j, 1, :, at], meta[j, 0, :, at])
                        best = jnp.maximum(best, row)
                        colmax[j, :, at] = jnp.maximum(colmax[j, :, at], col)
                rowmax[k % 2] = best

            @pl.loop(0, k // 2)
            def _(j):
                cross(2 * j, 2 * j + 1)

            @pl.when(k % 2 == 1)
            def _():
                cross(k - 1)

        finish(NCH - 1)

        half[2 * me_in_layer + c] = colmax[0, :, pl.ds(0, B)]

        @pl.loop(0, 16)
        def _(t):
            dx, dy = offset(t)
            hx, hy = (x - dx + 4) % 4, (y - dy + 4) % 4
            into = half.at[2 * me_in_layer + c]
            remote(colmax.at[t // 2, :, pl.ds(B, B)], into, s_half, r_half, place(hx, hy, z, 1 - c)).start()

            @pl.when(t > 0)
            def _():
                remote(colmax.at[t // 2, :, pl.ds(0, B)], into, s_half, r_half, place(hx, hy, z, c)).start()

        local_wait(half.at[pl.ds(0, 15)], r_half)

    @pl.when(jnp.logical_not(owner))
    def _():
        local_wait(half, r_half)

    whole[...] = jnp.max(half[...].reshape(8, 2, 1, B), axis=1)

    @pl.loop(1, 8)
    def _(t):
        remote(whole, back.at[pl.ds(64 - 8 * t, 8)], s_whole, r_whole, place(x, y, (z + t) % 8, c)).start()

    back[pl.ds(0, 8)] = whole[...]

    local_wait(idline, s_ids)

    @pl.loop(NCH - AHEAD, NCH)
    def _(q):
        sent(q)

    @pl.when(owner)
    def _():
        local_wait(idlayer.at[pl.ds(0, 7)], s_idl)
        local_wait(joint.at[:, pl.ds(0, B)], s_joint)
        local_wait(meta.at[:, :, :, pl.ds(0, B)], s_meta)
        local_wait(idsend.at[pl.ds(0, 31)], s_half)

    @pl.when(jnp.logical_not(owner))
    def _():
        local_wait(idlayer, s_idl)

    local_wait(back.at[pl.ds(8, 56)], r_whole)
    local_wait(back.at[pl.ds(8, 56)], s_whole)
    rest = back[:, 0, :]
    total = None
    for _ in range(3):
        term = rest.astype(BF16)
        rest = rest - term.astype(F32)
        found = jnp.dot(term, lanes[...], preferred_element_type=F32)
        total = found if total is None else total + found
    out_ref[...] = jnp.sum(total * hot[...], axis=0, keepdims=True).reshape(RD)


def on_device(embeddings, cluster_ids):
    dma = pltpu.SemaphoreType.DMA
    return pl.pallas_call(
        kernel,
        out_shape=jax.ShapeDtypeStruct((RD,), F32),
        in_specs=[pl.BlockSpec(memory_space=pltpu.HBM)] * 2,
        out_specs=pl.BlockSpec(memory_space=pltpu.VMEM),
        scratch_shapes=[
            pltpu.VMEM((RD,), jnp.int32),
            pltpu.VMEM((RD, D), BF16),
            pltpu.VMEM((G * 3, 8, D), BF16),
            pltpu.VMEM((G, 1, B), F32),
            pltpu.VMEM((7, 8, 1, B), F32),
            pltpu.VMEM((8, 1, B), F32),
            pltpu.VMEM((16, 1, B), F32),
            pltpu.VMEM((G, RD), F32),
            pltpu.VMEM((B, RD), BF16),
            pltpu.VMEM((2 * G * 3, 8, D), BF16),
            pltpu.VMEM((NCH, 2 * B, D), BF16),
            pltpu.VMEM((NCH, 2, 1, 2 * B), F32),
            pltpu.VMEM((NCH, 1, 2 * B), F32),
            pltpu.VMEM((16, 1, B), F32),
            pltpu.VMEM((8, 1, B), F32),
            pltpu.VMEM((G, 1, B), F32),
            pltpu.VMEM((2, B, 128), F32),
            pltpu.VMEM((2, B, 128), F32),
            pltpu.VMEM((2, B, 128), F32),
            pltpu.SemaphoreType.REGULAR, dma((2,)), dma((NCH,)), dma, dma, dma, dma, dma, dma,
            dma((NCH,)), dma, dma, dma((NCH,)), dma((NCH,)), dma, dma,
        ],
        compiler_params=pltpu.CompilerParams(
            collective_id=0, has_side_effects=True, vmem_limit_bytes=48 << 20
        ),
        name="semdedup",
    )(cluster_ids, embeddings)


def solution(mesh):
    placed = (P(("dp", "grp"), None), P(("dp", "grp")))
    return jax.shard_map(
        on_device, mesh=mesh, in_specs=placed, out_specs=P(("dp", "grp")), check_vma=False
    )
```

```python
import math

import jax
import jax.numpy as jnp
from jax import lax
from jax.experimental import pallas as pl
from jax.experimental.pallas import tpu as pltpu
from jax.sharding import PartitionSpec as P

D = 768
RD = 768
G = 64
CAP = 24
NCH = 8
SRC = 16
B = SRC * CAP
MESH = pl.DeviceIdType.MESH
F32, BF16 = jnp.float32, jnp.bfloat16


COLUMNS = (
    (0, 0), (2, 2), (1, 3), (3, 1), (1, 1), (3, 3), (0, 1), (0, 3),
    (1, 0), (3, 0), (0, 2), (2, 0), (1, 2), (3, 2), (2, 1), (2, 3),
)


def offset(t):
    def pick(which):
        out = jnp.int32(0)
        for n, xy in enumerate(COLUMNS):
            if xy[which]:
                out = jnp.where(t == n, xy[which], out)
        return out

    return pick(0), pick(1)


def lookup(dx, dy):
    out = jnp.zeros_like(dx)
    for n, xy in enumerate(COLUMNS):
        out = jnp.where((dx == xy[0]) & (dy == xy[1]), n, out)
    return out


def place(x, y, z, c):
    return ((y * 8 + z) * 2 + c, x)


def local_wait(ref, sem):
    pltpu.make_async_copy(ref, ref, sem).wait()


def pair_max(v, scale_col, id_col, scale_row, id_row, itself=None):
    row, cols = None, []
    for t in range(v.shape[1] // 128):
        at = slice(128 * t, 128 * (t + 1))
        same = id_col == id_row[:, at]
        if itself is not None:
            same = same & ~itself[:, at]
        m = jnp.where(same, v[:, at] * scale_col * scale_row[:, at], -1.0)
        row = m if row is None else jnp.maximum(row, m)
        cols.append(jnp.max(m, axis=0, keepdims=True))
    return row, jnp.concatenate(cols, axis=1)


def nt(a, b):
    return lax.dot_general(a, b, (((1,), (1,)), ((), ())), preferred_element_type=F32)


def kernel(
    ids_hbm, emb_hbm, out_ref,
    ids_ref, emb, send, idsend, idline, idlayer, idrecv, hot, lanes, recv, joint, meta, colmax, half, whole, back,
    scol, icol, rowmax,
    ready, s_in, s_rows, s_ids, s_idl, s_joint, s_meta, s_half, s_whole,
    r_rows, r_ids, r_idl, r_joint, r_meta, r_half, r_whole,
):
    dp, x = lax.axis_index("dp"), lax.axis_index("grp")
    y, z, c = dp // 16, (dp // 2) % 8, dp % 2
    zh, par = z // 2, z % 2
    owner = (x + y + z) % 2 == 0
    me_in_layer = x * 2 + y // 2
    other = place(x, y, z, 1 - c)

    def remote(src, dst, ssem, rsem, to):
        return pltpu.make_async_remote_copy(src, dst, ssem, rsem, device_id=to, device_id_type=MESH)

    def signal(sem, to):
        pl.semaphore_signal(sem, inc=1, device_id=to, device_id_type=MESH)

    get_ids = pltpu.make_async_copy(ids_hbm, ids_ref, s_in.at[0])
    get_ids.start()
    get_emb = pltpu.make_async_copy(emb_hbm, emb, s_in.at[1])
    get_emb.start()

    barrier = pltpu.get_barrier_semaphore()

    @pl.loop(1, 8)
    def _(t):
        signal(barrier, place(x, y, (z + t) % 8, c))

    @pl.when(owner)
    def _():
        signal(barrier, other)

        @pl.loop(1, 16)
        def _(t):
            signal(barrier, place((x + t // 4) % 4, (y + t) % 4, z, c))

    get_ids.wait()
    ids = ids_ref[...].reshape(1, RD)
    g = ids // 8
    gx, gy, gh = g // 16, (g // 4) & 3, g & 3
    col = lookup((gx - x) & 3, (gy - y) & 3)
    dh = (gh - zh) & 3
    line = ((2 * gh + ((gx + gy) & 1) - z) & 7) * 8 + gx * 2 + gy // 2
    mask = (lax.broadcasted_iota(jnp.int32, (G, RD), 0) == line).astype(F32)
    hot[...] = mask
    before = (
        lax.broadcasted_iota(jnp.int32, (RD, RD), 0) < lax.broadcasted_iota(jnp.int32, (RD, RD), 1)
    ).astype(F32).astype(BF16)
    counts = jnp.dot(mask.astype(BF16), before, preferred_element_type=F32)
    rank = jnp.sum(counts * mask, axis=0, keepdims=True).astype(jnp.int32)
    slot = (col * 4 + dh) * CAP + rank
    lane = ((col & 1) * 8 + dh * 2 + par) * CAP + rank
    at_lane = (lax.broadcasted_iota(jnp.int32, (B, RD), 0) == lane).astype(F32).astype(BF16)
    lanes[...] = at_lane
    idsend[:, 0, :] = nt((mask * ((ids & 7) + 1).astype(F32)).astype(BF16), at_lane)

    get_emb.wait()

    @pl.loop(0, NCH)
    def _(q):
        pick = lax.broadcasted_iota(jnp.int32, (8 * CAP, RD), 0) + q * (8 * CAP) == slot
        rows = jnp.dot(pick.astype(F32).astype(BF16), emb[...], preferred_element_type=F32)
        send[pl.ds(q * 24, 24)] = rows.astype(BF16).reshape(24, 8, D)

    pl.semaphore_wait(barrier, 15)

    @pl.loop(1, 8)
    def _(t):
        signal(ready, place(x, y, (z + t) % 8, c))

    @pl.loop(1, 8)
    def _(t):
        remote(idsend.at[pl.ds(8 * t, 8)], idline.at[t - 1], s_ids, r_ids, place(x, y, (z + t) % 8, c)).start()

    def row_copy(i):
        dx, dy = offset(i // 4)
        tx, ty, tz = (x + dx) % 4, (y + dy) % 4, 2 * ((zh + i) % 4)
        tz = tz + (tx + ty) % 2
        k, at = i // 8, 2 * i + par
        copy = remote(
            send.at[pl.ds(3 * i, 3)], recv.at[pl.ds(3 * at, 3)], s_rows, r_rows.at[k], place(tx, ty, tz, c)
        )
        return copy, jnp.logical_or(i < 4, tz == z)

    @pl.when(owner)
    def _():
        pltpu.make_async_copy(send.at[pl.ds(0, 3)], recv.at[pl.ds(3 * par, 3)], r_rows.at[0]).start()

    @pl.loop(0, 4)
    def _(i):
        @pl.when(jnp.logical_not(jnp.logical_and(owner, i == 0)))
        def _():
            row_copy(i)[0].start()

    @pl.loop(1, 16)
    def _(t):
        copy, near = row_copy(4 * t)

        @pl.when(near)
        def _():
            copy.start()

    pl.semaphore_wait(ready, 7)

    @pl.loop(0, G)
    def _(n):
        copy, near = row_copy(n)

        @pl.when(jnp.logical_not(near))
        def _():
            copy.start()

    local_wait(idline, r_ids)
    idlayer[...] = jnp.maximum(idsend[pl.ds(0, 8)], jnp.max(idline[...], axis=0))

    @pl.loop(0, 16)
    def _(t):
        dx, dy = offset(t)
        tx, ty = (x + dx) % 4, (y + dy) % 4

        @pl.when(jnp.logical_and((tx + ty + z) % 2 == 0, t > 0))
        def _():
            remote(idlayer.at[tx * 2 + ty // 2], idrecv.at[t], s_idl, r_idl, place(tx, ty, z, c)).start()

    @pl.when(owner)
    def _():
        colmax[...] = jnp.full(colmax.shape, -1.0, F32)
        idrecv[0] = idlayer[me_in_layer]
        local_wait(idrecv.at[pl.ds(1, 15)], r_idl)

        def finish(k):
            local_wait(joint.at[k, pl.ds(B, B)], r_joint.at[k])
            local_wait(meta.at[k, :, :, pl.ds(B, B)], r_meta.at[k])
            v = nt(joint[k, pl.ds(0, B), :], joint[k, pl.ds(B, B), :])
            at = pl.ds(B, B)
            row, _ = pair_max(v, scol[k % 2], icol[k % 2], meta[k, 1, :, at], meta[k, 0, :, at])
            row = jnp.maximum(rowmax[k % 2], row)
            best = jnp.max(row.T, axis=0, keepdims=True)
            colmax[k, :, pl.ds(0, B)] = jnp.maximum(colmax[k, :, pl.ds(0, B)], best)

        @pl.loop(0, NCH)
        def _(k):
            chunk = recv.at[pl.ds(k * 48, 48)]
            local_wait(chunk, r_rows.at[k])
            joint[k, pl.ds(0, B), :] = chunk[...].reshape(B, D)
            remote(joint.at[k, pl.ds(0, B)], joint.at[k, pl.ds(B, B)], s_joint, r_joint.at[k], other).start()
            id_row = jnp.maximum(idrecv[2 * k], idrecv[2 * k + 1])
            mine = joint[k, pl.ds(0, B), :]
            gram = nt(mine, mine)
            eye = lax.broadcasted_iota(jnp.int32, (B, B), 0) == lax.broadcasted_iota(jnp.int32, (B, B), 1)
            squares = jnp.where(eye, gram, 0.0)
            scale_row = lax.rsqrt(jnp.sum(squares, axis=0, keepdims=True) / D + 1e-6) / math.sqrt(D)
            scale_col = lax.rsqrt(jnp.sum(squares, axis=1, keepdims=True) / D + 1e-6) / math.sqrt(D)
            id_col = jnp.sum(jnp.where(eye, id_row, 0.0), axis=1, keepdims=True)
            meta[k, 0, :, pl.ds(0, B)] = id_row
            meta[k, 1, :, pl.ds(0, B)] = scale_row
            remote(
                meta.at[k, :, :, pl.ds(0, B)], meta.at[k, :, :, pl.ds(B, B)], s_meta, r_meta.at[k], other
            ).start()
            scol[k % 2] = jnp.broadcast_to(scale_col, (B, 128))
            icol[k % 2] = jnp.broadcast_to(id_col, (B, 128))
            row, _ = pair_max(gram, scol[k % 2], icol[k % 2], scale_row, id_row, eye)
            rowmax[k % 2] = row

            @pl.when(k > 0)
            def _():
                finish(k - 1)

            def cross(*chunks):
                best = rowmax[k % 2]
                for j in chunks:
                    for n in range(3):
                        at = pl.ds(256 * n, 256)
                        v = nt(joint[k, pl.ds(0, B), :], joint[j, at, :])
                        row, col = pair_max(v, scol[k % 2], icol[k % 2], meta[j, 1, :, at], meta[j, 0, :, at])
                        best = jnp.maximum(best, row)
                        colmax[j, :, at] = jnp.maximum(colmax[j, :, at], col)
                rowmax[k % 2] = best

            @pl.loop(0, k // 4)
            def _(j):
                cross(4 * j, 4 * j + 1, 4 * j + 2, 4 * j + 3)

            @pl.when(k % 4 >= 2)
            def _():
                cross(k // 4 * 4, k // 4 * 4 + 1)

            @pl.when(k % 2 == 1)
            def _():
                cross(k - 1)

        finish(NCH - 1)

        half[2 * me_in_layer + c] = colmax[0, :, pl.ds(0, B)]

        into = half.at[2 * me_in_layer + c]
        for t, (dx, dy) in enumerate(COLUMNS):
            hx, hy = (x + 4 - dx) % 4, (y + 4 - dy) % 4
            remote(colmax.at[t // 2, :, pl.ds(B, B)], into, s_half, r_half, place(hx, hy, z, 1 - c)).start()
            if t > 0:
                remote(colmax.at[t // 2, :, pl.ds(0, B)], into, s_half, r_half, place(hx, hy, z, c)).start()

        local_wait(half.at[pl.ds(0, 15)], r_half)

    @pl.when(jnp.logical_not(owner))
    def _():
        local_wait(half, r_half)

    whole[...] = jnp.max(half[...].reshape(8, 2, 1, B), axis=1)

    for t in (4, 3, 5, 2, 6, 1, 7):
        remote(whole, back.at[pl.ds(64 - 8 * t, 8)], s_whole, r_whole, place(x, y, (z + t) % 8, c)).start()

    back[pl.ds(0, 8)] = whole[...]

    local_wait(idline, s_ids)

    @pl.when(owner)
    def _():
        local_wait(send.at[pl.ds(0, 189)], s_rows)
        local_wait(idlayer.at[pl.ds(0, 7)], s_idl)
        local_wait(joint.at[:, pl.ds(0, B)], s_joint)
        local_wait(meta.at[:, :, :, pl.ds(0, B)], s_meta)
        local_wait(idsend.at[pl.ds(0, 31)], s_half)

    @pl.when(jnp.logical_not(owner))
    def _():
        local_wait(send, s_rows)
        local_wait(idlayer, s_idl)

    local_wait(back.at[pl.ds(8, 56)], r_whole)
    local_wait(back.at[pl.ds(8, 56)], s_whole)
    rest = back[:, 0, :]
    total = None
    for _ in range(3):
        term = rest.astype(BF16)
        rest = rest - term.astype(F32)
        found = jnp.dot(term, lanes[...], preferred_element_type=F32)
        total = found if total is None else total + found
    out_ref[...] = jnp.sum(total * hot[...], axis=0, keepdims=True).reshape(RD)


def on_device(embeddings, cluster_ids):
    dma = pltpu.SemaphoreType.DMA
    return pl.pallas_call(
        kernel,
        out_shape=jax.ShapeDtypeStruct((RD,), F32),
        in_specs=[pl.BlockSpec(memory_space=pltpu.HBM)] * 2,
        out_specs=pl.BlockSpec(memory_space=pltpu.VMEM),
        scratch_shapes=[
            pltpu.VMEM((RD,), jnp.int32),
            pltpu.VMEM((RD, D), BF16),
            pltpu.VMEM((G * 3, 8, D), BF16),
            pltpu.VMEM((G, 1, B), F32),
            pltpu.VMEM((7, 8, 1, B), F32),
            pltpu.VMEM((8, 1, B), F32),
            pltpu.VMEM((16, 1, B), F32),
            pltpu.VMEM((G, RD), F32),
            pltpu.VMEM((B, RD), BF16),
            pltpu.VMEM((2 * G * 3, 8, D), BF16),
            pltpu.VMEM((NCH, 2 * B, D), BF16),
            pltpu.VMEM((NCH, 2, 1, 2 * B), F32),
            pltpu.VMEM((NCH, 1, 2 * B), F32),
            pltpu.VMEM((16, 1, B), F32),
            pltpu.VMEM((8, 1, B), F32),
            pltpu.VMEM((G, 1, B), F32),
            pltpu.VMEM((2, B, 128), F32),
            pltpu.VMEM((2, B, 128), F32),
            pltpu.VMEM((2, B, 128), F32),
            pltpu.SemaphoreType.REGULAR, dma((2,)), dma, dma, dma, dma, dma, dma, dma,
            dma((NCH,)), dma, dma, dma((NCH,)), dma((NCH,)), dma, dma,
        ],
        compiler_params=pltpu.CompilerParams(
            collective_id=0, has_side_effects=True, vmem_limit_bytes=48 << 20
        ),
        name="semdedup",
    )(cluster_ids, embeddings)


def solution(mesh):
    placed = (P(("dp", "grp"), None), P(("dp", "grp")))
    return jax.shard_map(
        on_device, mesh=mesh, in_specs=placed, out_specs=P(("dp", "grp")), check_vma=False
    )
```

```python
import math

import jax
import jax.numpy as jnp
from jax import lax
from jax.experimental import pallas as pl
from jax.experimental.pallas import tpu as pltpu
from jax.sharding import PartitionSpec as P

D = 768
RD = 768
G = 64
CAP = 24
NCH = 8
SRC = 16
B = SRC * CAP
MESH = pl.DeviceIdType.MESH
F32, BF16 = jnp.float32, jnp.bfloat16


COLUMNS = (
    (0, 0), (2, 2), (1, 3), (3, 1), (1, 1), (3, 3), (0, 1), (0, 3),
    (1, 0), (3, 0), (0, 2), (2, 0), (1, 2), (3, 2), (2, 1), (2, 3),
)


def offset(t):
    def pick(which):
        out = jnp.int32(0)
        for n, xy in enumerate(COLUMNS):
            if xy[which]:
                out = jnp.where(t == n, xy[which], out)
        return out

    return pick(0), pick(1)


def lookup(dx, dy):
    out = jnp.zeros_like(dx)
    for n, xy in enumerate(COLUMNS):
        out = jnp.where((dx == xy[0]) & (dy == xy[1]), n, out)
    return out


def place(x, y, z, c):
    return ((y * 8 + z) * 2 + c, x)


def local_wait(ref, sem):
    pltpu.make_async_copy(ref, ref, sem).wait()


def pair_max(v, scale_col, id_col, scale_row, id_row, itself=None):
    row, cols = None, []
    for t in range(v.shape[1] // 128):
        at = slice(128 * t, 128 * (t + 1))
        same = id_col == id_row[:, at]
        if itself is not None:
            same = same & ~itself[:, at]
        m = jnp.where(same, v[:, at] * scale_col * scale_row[:, at], -1.0)
        row = m if row is None else jnp.maximum(row, m)
        cols.append(jnp.max(m, axis=0, keepdims=True))
    return row, jnp.concatenate(cols, axis=1)


def nt(a, b):
    return lax.dot_general(a, b, (((1,), (1,)), ((), ())), preferred_element_type=F32)


def kernel(
    ids_hbm, emb_hbm, out_ref,
    ids_ref, emb, send, idsend, idline, idlayer, idrecv, hot, lanes, recv, joint, meta, colmax, half, whole, back,
    scol, icol, rowmax,
    ready, s_in, s_rows, s_ids, s_idl, s_joint, s_meta, s_half, s_whole,
    r_rows, r_ids, r_idl, r_joint, r_meta, r_half, r_whole,
):
    dp, x = lax.axis_index("dp"), lax.axis_index("grp")
    y, z, c = dp // 16, (dp // 2) % 8, dp % 2
    zh, par = z // 2, z % 2
    owner = (x + y + z) % 2 == 0
    me_in_layer = x * 2 + y // 2
    other = place(x, y, z, 1 - c)

    def remote(src, dst, ssem, rsem, to):
        return pltpu.make_async_remote_copy(src, dst, ssem, rsem, device_id=to, device_id_type=MESH)

    def signal(sem, to):
        pl.semaphore_signal(sem, inc=1, device_id=to, device_id_type=MESH)

    get_ids = pltpu.make_async_copy(ids_hbm, ids_ref, s_in.at[0])
    get_ids.start()
    get_emb = pltpu.make_async_copy(emb_hbm, emb, s_in.at[1])
    get_emb.start()

    barrier = pltpu.get_barrier_semaphore()

    @pl.loop(1, 8)
    def _(t):
        signal(barrier, place(x, y, (z + t) % 8, c))

    @pl.when(owner)
    def _():
        signal(barrier, other)

        @pl.loop(1, 16)
        def _(t):
            signal(barrier, place((x + t // 4) % 4, (y + t) % 4, z, c))

    get_ids.wait()
    ids = ids_ref[...].reshape(1, RD)
    g = ids // 8
    gx, gy, gh = g // 16, (g // 4) & 3, g & 3
    col = lookup((gx - x) & 3, (gy - y) & 3)
    dh = (gh - zh) & 3
    line = ((2 * gh + ((gx + gy) & 1) - z) & 7) * 8 + gx * 2 + gy // 2
    mask = (lax.broadcasted_iota(jnp.int32, (G, RD), 0) == line).astype(F32)
    hot[...] = mask
    before = (
        lax.broadcasted_iota(jnp.int32, (RD, RD), 0) < lax.broadcasted_iota(jnp.int32, (RD, RD), 1)
    ).astype(F32).astype(BF16)
    counts = jnp.dot(mask.astype(BF16), before, preferred_element_type=F32)
    rank = jnp.sum(counts * mask, axis=0, keepdims=True).astype(jnp.int32)
    slot = (col * 4 + dh) * CAP + rank
    lane = ((col & 1) * 8 + dh * 2 + par) * CAP + rank
    at_lane = (lax.broadcasted_iota(jnp.int32, (B, RD), 0) == lane).astype(F32).astype(BF16)
    lanes[...] = at_lane
    idsend[:, 0, :] = nt((mask * ((ids & 7) + 1).astype(F32)).astype(BF16), at_lane)

    get_emb.wait()

    @pl.loop(0, NCH // 2)
    def _(q):
        pick = lax.broadcasted_iota(jnp.int32, (8 * CAP, RD), 0) + q * (8 * CAP) == slot
        rows = jnp.dot(pick.astype(F32).astype(BF16), emb[...], preferred_element_type=F32)
        send[pl.ds(q * 24, 24)] = rows.astype(BF16).reshape(24, 8, D)

    pl.semaphore_wait(barrier, 15)

    @pl.loop(1, 8)
    def _(t):
        signal(ready, place(x, y, (z + t) % 8, c))

    @pl.loop(1, 8)
    def _(t):
        remote(idsend.at[pl.ds(8 * t, 8)], idline.at[t - 1], s_ids, r_ids, place(x, y, (z + t) % 8, c)).start()

    @pl.loop(NCH // 2, NCH)
    def _(q):
        pick = lax.broadcasted_iota(jnp.int32, (8 * CAP, RD), 0) + q * (8 * CAP) == slot
        rows = jnp.dot(pick.astype(F32).astype(BF16), emb[...], preferred_element_type=F32)
        send[pl.ds(q * 24, 24)] = rows.astype(BF16).reshape(24, 8, D)

    def row_copy(i):
        dx, dy = offset(i // 4)
        tx, ty, tz = (x + dx) % 4, (y + dy) % 4, 2 * ((zh + i) % 4)
        tz = tz + (tx + ty) % 2
        k, at = i // 8, 2 * i + par
        copy = remote(
            send.at[pl.ds(3 * i, 3)], recv.at[pl.ds(3 * at, 3)], s_rows, r_rows.at[k], place(tx, ty, tz, c)
        )
        return copy, jnp.logical_or(i < 4, tz == z)

    @pl.when(owner)
    def _():
        pltpu.make_async_copy(send.at[pl.ds(0, 3)], recv.at[pl.ds(3 * par, 3)], r_rows.at[0]).start()

    @pl.loop(0, 4)
    def _(i):
        @pl.when(jnp.logical_not(jnp.logical_and(owner, i == 0)))
        def _():
            row_copy(i)[0].start()

    @pl.loop(1, 16)
    def _(t):
        copy, near = row_copy(4 * t)

        @pl.when(near)
        def _():
            copy.start()

    pl.semaphore_wait(ready, 7)

    @pl.loop(0, G)
    def _(n):
        copy, near = row_copy(n)

        @pl.when(jnp.logical_not(near))
        def _():
            copy.start()

    local_wait(idline, r_ids)
    idlayer[...] = jnp.maximum(idsend[pl.ds(0, 8)], jnp.max(idline[...], axis=0))

    @pl.loop(0, 16)
    def _(t):
        dx, dy = offset(t)
        tx, ty = (x + dx) % 4, (y + dy) % 4

        @pl.when(jnp.logical_and((tx + ty + z) % 2 == 0, t > 0))
        def _():
            remote(idlayer.at[tx * 2 + ty // 2], idrecv.at[t], s_idl, r_idl, place(tx, ty, z, c)).start()

    @pl.when(owner)
    def _():
        colmax[...] = jnp.full(colmax.shape, -1.0, F32)
        idrecv[0] = idlayer[me_in_layer]
        local_wait(idrecv.at[pl.ds(1, 15)], r_idl)

        def finish(k):
            local_wait(joint.at[k, pl.ds(B, B)], r_joint.at[k])
            local_wait(meta.at[k, :, :, pl.ds(B, B)], r_meta.at[k])
            v = nt(joint[k, pl.ds(0, B), :], joint[k, pl.ds(B, B), :])
            at = pl.ds(B, B)
            row, _ = pair_max(v, scol[k % 2], icol[k % 2], meta[k, 1, :, at], meta[k, 0, :, at])
            row = jnp.maximum(rowmax[k % 2], row)
            best = jnp.max(row.T, axis=0, keepdims=True)
            colmax[k, :, pl.ds(0, B)] = jnp.maximum(colmax[k, :, pl.ds(0, B)], best)

        @pl.loop(0, NCH)
        def _(k):
            @pl.when(k > 0)
            def _():
                finish(k - 1)

            chunk = recv.at[pl.ds(k * 48, 48)]
            local_wait(chunk, r_rows.at[k])
            joint[k, pl.ds(0, B), :] = chunk[...].reshape(B, D)
            remote(joint.at[k, pl.ds(0, B)], joint.at[k, pl.ds(B, B)], s_joint, r_joint.at[k], other).start()
            id_row = jnp.maximum(idrecv[2 * k], idrecv[2 * k + 1])
            mine = joint[k, pl.ds(0, B), :]
            gram = nt(mine, mine)
            eye = lax.broadcasted_iota(jnp.int32, (B, B), 0) == lax.broadcasted_iota(jnp.int32, (B, B), 1)
            squares = jnp.where(eye, gram, 0.0)
            scale_row = lax.rsqrt(jnp.sum(squares, axis=0, keepdims=True) / D + 1e-6) / math.sqrt(D)
            scale_col = lax.rsqrt(jnp.sum(squares, axis=1, keepdims=True) / D + 1e-6) / math.sqrt(D)
            id_col = jnp.sum(jnp.where(eye, id_row, 0.0), axis=1, keepdims=True)
            meta[k, 0, :, pl.ds(0, B)] = id_row
            meta[k, 1, :, pl.ds(0, B)] = scale_row
            remote(
                meta.at[k, :, :, pl.ds(0, B)], meta.at[k, :, :, pl.ds(B, B)], s_meta, r_meta.at[k], other
            ).start()
            scol[k % 2] = jnp.broadcast_to(scale_col, (B, 128))
            icol[k % 2] = jnp.broadcast_to(id_col, (B, 128))
            row, _ = pair_max(gram, scol[k % 2], icol[k % 2], scale_row, id_row, eye)
            rowmax[k % 2] = row

            def cross(*chunks):
                best = rowmax[k % 2]
                for j in chunks:
                    for n in range(3):
                        at = pl.ds(256 * n, 256)
                        v = nt(joint[k, pl.ds(0, B), :], joint[j, at, :])
                        row, col = pair_max(v, scol[k % 2], icol[k % 2], meta[j, 1, :, at], meta[j, 0, :, at])
                        best = jnp.maximum(best, row)
                        colmax[j, :, at] = jnp.maximum(colmax[j, :, at], col)
                rowmax[k % 2] = best

            @pl.loop(0, k // 4)
            def _(j):
                cross(4 * j, 4 * j + 1, 4 * j + 2, 4 * j + 3)

            @pl.when(k % 4 >= 2)
            def _():
                cross(k // 4 * 4, k // 4 * 4 + 1)

            @pl.when(k % 2 == 1)
            def _():
                cross(k - 1)

        finish(NCH - 1)

        half[2 * me_in_layer + c] = colmax[0, :, pl.ds(0, B)]

        into = half.at[2 * me_in_layer + c]
        for t, (dx, dy) in enumerate(COLUMNS):
            hx, hy = (x + 4 - dx) % 4, (y + 4 - dy) % 4
            remote(colmax.at[t // 2, :, pl.ds(B, B)], into, s_half, r_half, place(hx, hy, z, 1 - c)).start()
            if t > 0:
                remote(colmax.at[t // 2, :, pl.ds(0, B)], into, s_half, r_half, place(hx, hy, z, c)).start()

        local_wait(half.at[pl.ds(0, 15)], r_half)

    @pl.when(jnp.logical_not(owner))
    def _():
        local_wait(half, r_half)

    whole[...] = jnp.max(half[...].reshape(8, 2, 1, B), axis=1)

    for t in (4, 3, 5, 2, 6, 1, 7):
        remote(whole, back.at[pl.ds(64 - 8 * t, 8)], s_whole, r_whole, place(x, y, (z + t) % 8, c)).start()

    back[pl.ds(0, 8)] = whole[...]

    local_wait(idline, s_ids)

    @pl.when(owner)
    def _():
        local_wait(send.at[pl.ds(0, 189)], s_rows)
        local_wait(idlayer.at[pl.ds(0, 7)], s_idl)
        local_wait(joint.at[:, pl.ds(0, B)], s_joint)
        local_wait(meta.at[:, :, :, pl.ds(0, B)], s_meta)
        local_wait(idsend.at[pl.ds(0, 31)], s_half)

    @pl.when(jnp.logical_not(owner))
    def _():
        local_wait(send, s_rows)
        local_wait(idlayer, s_idl)

    local_wait(back.at[pl.ds(8, 56)], r_whole)
    local_wait(back.at[pl.ds(8, 56)], s_whole)
    rest = back[:, 0, :]
    total = None
    for _ in range(3):
        term = rest.astype(BF16)
        rest = rest - term.astype(F32)
        found = jnp.dot(term, lanes[...], preferred_element_type=F32)
        total = found if total is None else total + found
    out_ref[...] = jnp.sum(total * hot[...], axis=0, keepdims=True).reshape(RD)


def on_device(embeddings, cluster_ids):
    dma = pltpu.SemaphoreType.DMA
    return pl.pallas_call(
        kernel,
        out_shape=jax.ShapeDtypeStruct((RD,), F32),
        in_specs=[pl.BlockSpec(memory_space=pltpu.HBM)] * 2,
        out_specs=pl.BlockSpec(memory_space=pltpu.VMEM),
        scratch_shapes=[
            pltpu.VMEM((RD,), jnp.int32),
            pltpu.VMEM((RD, D), BF16),
            pltpu.VMEM((G * 3, 8, D), BF16),
            pltpu.VMEM((G, 1, B), F32),
            pltpu.VMEM((7, 8, 1, B), F32),
            pltpu.VMEM((8, 1, B), F32),
            pltpu.VMEM((16, 1, B), F32),
            pltpu.VMEM((G, RD), F32),
            pltpu.VMEM((B, RD), BF16),
            pltpu.VMEM((2 * G * 3, 8, D), BF16),
            pltpu.VMEM((NCH, 2 * B, D), BF16),
            pltpu.VMEM((NCH, 2, 1, 2 * B), F32),
            pltpu.VMEM((NCH, 1, 2 * B), F32),
            pltpu.VMEM((16, 1, B), F32),
            pltpu.VMEM((8, 1, B), F32),
            pltpu.VMEM((G, 1, B), F32),
            pltpu.VMEM((2, B, 128), F32),
            pltpu.VMEM((2, B, 128), F32),
            pltpu.VMEM((2, B, 128), F32),
            pltpu.SemaphoreType.REGULAR, dma((2,)), dma, dma, dma, dma, dma, dma, dma,
            dma((NCH,)), dma, dma, dma((NCH,)), dma((NCH,)), dma, dma,
        ],
        compiler_params=pltpu.CompilerParams(
            collective_id=0, has_side_effects=True, vmem_limit_bytes=48 << 20
        ),
        name="semdedup",
    )(cluster_ids, embeddings)


def solution(mesh):
    placed = (P(("dp", "grp"), None), P(("dp", "grp")))
    return jax.shard_map(
        on_device, mesh=mesh, in_specs=placed, out_specs=P(("dp", "grp")), check_vma=False
    )
```
